128 devices in a mesh: tp: 4 (over z_lo, core), cp: 32 (over y, x, z_hi).
Axes of the slice: x: 4, y: 4, z: 4 (z_hi: 2, z_lo: 2; z = z_hi * 2 + z_lo), core: 2. Of those that a mesh axis runs over, the one named last changes fastest.
Arguments:
- queries: bfloat16 [12288, 32, 128], P('cp', 'tp')
- keys: bfloat16 [12288, 8, 128], P('cp', 'tp')
- values: bfloat16 [12288, 8, 128], P('cp', 'tp'), may hold values from -6 to 6
- positions: int32 [12288], P('cp'), may hold values from 0 to 12287, as said below
Outputs:
- attended: bfloat16 [12288, 32, 128], P('cp', 'tp')
The draws below stay inside these ranges and needn't reach their ends.
Inputs may be any that keep to these rules, and one draw needn't show every extreme that they name: positions is a permutation of the 12288 positions made of blocks of 192 consecutive ascending positions, each block starting at a multiple of 192 and stored in 192 consecutive rows starting at a multiple of 192; which block lies where is drawn from the seed.
All inputs are finite; a program needn't handle non-finite values.
Results may differ from the reference program's by a relative error of at most 0.0055.
Values may be sent and summed in bfloat16 or wider, within the bound.
A program may use at most 320 MiB of HBM per device.

```python
import jax
import jax.numpy as jnp
from jax import lax

QUERY_HEADS = 32
KEY_VALUE_HEADS = 8
HEAD_WIDTH = 128
TOK_DEV = 384
SPAN = 192
SEQUENCE_TOKENS = 12288
N_CP = 32


def base_row_block(key, heads):
    return jnp.clip(1.7 * jax.random.normal(key, (SEQUENCE_TOKENS, heads, HEAD_WIDTH), jnp.float32), -8.0, 8.0)


def draw_keys(key, part):
    key = jax.random.fold_in(key, 1)
    base_offset = base_row_block(key, KEY_VALUE_HEADS)
    return base_offset.astype(jnp.bfloat16)


def draw_queries(key, part):
    key = jax.random.fold_in(key, 2)
    base_offset = base_row_block(key, QUERY_HEADS)
    return base_offset.astype(jnp.bfloat16)


def draw_positions(key, part):
    key = jax.random.fold_in(key, 3)
    order = jax.random.permutation(key, 2 * N_CP).astype(jnp.int32)
    inside = jnp.arange(SPAN, dtype=jnp.int32)
    return (order[:, None] * SPAN + inside[None, :]).reshape(SEQUENCE_TOKENS)


def shard_levels(own_key, shape, pieces, least, high):
    def one(position, shards_of):
        draws = jax.random.uniform(jax.random.fold_in(jax.random.fold_in(own_key, 6), position), (shards_of,), jnp.float32, least / len(pieces), high / len(pieces))
        return jnp.repeat(jnp.exp(draws), shape[position] // shards_of).reshape((-1,) + (1,) * (len(shape) - position - 1))

    loudness = one(*pieces[0])
    for cut in pieces[1:]:
        loudness = loudness * one(*cut)
    return loudness


def centred(rng, dims, scale, limit, shards=(), kind=jnp.bfloat16):
    values = scale * jax.random.normal(rng, dims, jnp.float32)
    if shards:
        values = values * shard_levels(rng, dims, shards, -0.22, 0.18)
    return jnp.clip(values, -limit, limit).astype(kind)


def setup_inputs(seed: int = 0) -> dict:
    splits = jax.random.split(jax.random.key(seed), 5)
    return {
        "queries": draw_queries(jax.random.fold_in(splits[4], 71), 0),
        "keys": draw_keys(jax.random.fold_in(splits[4], 71), 0),
        "values": centred(splits[2], (SEQUENCE_TOKENS, KEY_VALUE_HEADS, HEAD_WIDTH), 1.0, 6.0, ((0, 32), (1, 4))),
        "positions": draw_positions(jax.random.fold_in(splits[4], 71), 0),
    }


def reference(queries, keys, values, positions):
    query_group = QUERY_HEADS // KEY_VALUE_HEADS
    scale = HEAD_WIDTH ** -0.5
    grouped_queries = queries.reshape(SEQUENCE_TOKENS, KEY_VALUE_HEADS, query_group, HEAD_WIDTH)
    keys_wide = keys.astype(jnp.float32)
    values_wide = values.astype(jnp.float32)

    def one_block(index):
        start = (index * TOK_DEV).astype(jnp.int32)
        block = lax.dynamic_slice_in_dim(grouped_queries, start, TOK_DEV, 0).astype(jnp.float32)
        block_pos = lax.dynamic_slice_in_dim(positions, start, TOK_DEV, 0)
        score = jnp.einsum("qgrd,kgd->grqk", block, keys_wide) * scale
        visible = block_pos[:, None] >= positions[None, :]
        score = jnp.where(visible[None, None], score, -jnp.inf)
        peak = jnp.max(score, axis=-1, keepdims=True)
        expo = jnp.exp(score - peak)
        total = jnp.sum(expo, axis=-1)
        weight = expo.astype(jnp.bfloat16)
        weight = lax.optimization_barrier(weight).astype(jnp.float32)
        summed = jnp.einsum("grqk,kgd->qgrd", weight, values_wide)
        result = summed / jnp.transpose(total, (2, 0, 1))[..., None]
        return result.reshape(TOK_DEV, QUERY_HEADS, HEAD_WIDTH).astype(jnp.bfloat16)

    blocks = lax.map(one_block, jnp.arange(N_CP, dtype=jnp.int32))
    return blocks.reshape(SEQUENCE_TOKENS, QUERY_HEADS, HEAD_WIDTH)
```

```python
import jax
import jax.numpy as jnp
from jax import lax
from jax.experimental import pallas as pl
from jax.experimental.pallas import tpu as pltpu
from jax.sharding import PartitionSpec as P

MESH = pl.DeviceIdType.MESH
F32 = jnp.float32
BF16 = jnp.bfloat16

SPAN = 192
TOK = 2 * SPAN
GROUP = 4
WIDTH = 128
ROWS = GROUP * SPAN
KROWS = TOK + 16
BIG = 1e30
SCALE = WIDTH**-0.5 * 1.4426950408889634

ORDER = [
    (0, 0),
    (-1, 0), (1, 0), (0, -1), (0, 1),
    (2, 0), (0, 2),
    (-1, -1), (1, 1), (-1, 1), (1, -1),
    (2, -1), (-1, 2), (2, 1), (1, 2),
    (2, 2),
]
SLOT = {place: n for n, place in enumerate(ORDER)}
UNITS = len(ORDER)


def wrap(d):
    return (d + 1) % 4 - 1


def forwards(kind, place):
    first, second = (0, 1) if kind == 0 else (1, 0)
    sends = []

    def send(axis, direction, half):
        there = list(place)
        there[axis] = wrap(there[axis] - direction)
        sends.append((axis, direction, half, SLOT[tuple(there)]))

    if place[second] == 0:
        d = place[first]
        if d == 0:
            send(first, 1, None)
            send(first, -1, None)
        elif d == -1:
            send(first, 1, 0)
        elif d == 1:
            send(first, -1, 1)
        send(second, 1, None)
        send(second, -1, None)
    elif place[second] == -1:
        send(second, 1, 0)
    elif place[second] == 1:
        send(second, -1, 1)
    return sends


def in_halves(kind, place):
    first, second = (0, 1) if kind == 0 else (1, 0)
    return place[second] == 2 or (place[second] == 0 and place[first] == 2)


SENDS = {}
for _kind in range(2):
    for _place in ORDER:
        for _k, _s in enumerate(forwards(_kind, _place)):
            SENDS[(_kind, SLOT[_place], _k)] = len([key for key in SENDS if key[0] == _kind])
N_SENDS = len(SENDS) // 2


def kernel(
    q_ref, k_ref, v_ref, o_ref,
    kbuf, vbuf, qx, qz, oz,
    acc0, acc1, m0, m1, l0, l1, s0, s1, c0, c1,
    send_sem, recv_sem, zsend_sem, zrecv_sem,
):
    accs, maxs, sums = (acc0, acc1), (m0, m1), (l0, l1)
    scores, peaks = (s0, s1), (c0, c1)
    cp = lax.axis_index("cp")
    y, x, z = cp // 8, (cp // 2) % 4, cp % 2
    other = 1 - z

    def device(axis, direction):
        if axis == 0:
            return (y * 4 + (x + direction + 4) % 4) * 2 + z
        return (((y + direction + 4) % 4) * 4 + x) * 2 + z

    partner = (y * 4 + x) * 2 + other

    def part(kind, half):
        if kind == 0:
            return (slice(0, KROWS), slice(0, SPAN), slice(SPAN, KROWS))[0 if half is None else half + 1]
        return (slice(0, WIDTH), slice(0, WIDTH // 2), slice(WIDTH // 2, WIDTH))[0 if half is None else half + 1]

    def view(kind, slot, half):
        buf = kbuf if kind == 0 else vbuf
        return buf.at[slot, part(kind, half)]

    def send_copy(wave, kind, n, k, sends):
        axis, direction, half, there = sends[k]
        if wave == 0 and n == 0:
            src = (k_ref if kind == 0 else v_ref).at[z]
        else:
            src = view(kind, wave * UNITS + n, half)
        return pltpu.make_async_remote_copy(
            src_ref=src,
            dst_ref=view(kind, wave * UNITS + there, half),
            send_sem=send_sem.at[wave, kind, SENDS[(kind, n, k)]],
            recv_sem=recv_sem.at[wave, kind, there, 0 if half is None else half],
            device_id={"cp": device(axis, direction)},
            device_id_type=MESH,
        )

    def forward(wave, n):
        for kind in range(2):
            sends = forwards(kind, ORDER[n])
            for k in range(len(sends)):
                send_copy(wave, kind, n, k, sends).start()

    def arrive(wave, n):
        for kind in range(2):
            for half in (0, 1) if in_halves(kind, ORDER[n]) else (None,):
                here = view(kind, wave * UNITS + n, half)
                pltpu.make_async_remote_copy(
                    src_ref=here,
                    dst_ref=here,
                    send_sem=send_sem.at[wave, kind, 0],
                    recv_sem=recv_sem.at[wave, kind, n, 0 if half is None else half],
                    device_id={"cp": partner},
                    device_id_type=MESH,
                ).wait_recv()
            sends = forwards(kind, ORDER[n])
            for k in range(len(sends)):
                send_copy(wave, kind, n, k, sends).start()

    def z_copy(i):
        src, dst = (
            (k_ref.at[other], kbuf.at[UNITS]),
            (v_ref.at[other], vbuf.at[UNITS]),
            (q_ref.at[other], qz),
            (oz, o_ref.at[z]),
        )[i]
        return pltpu.make_async_remote_copy(
            src_ref=src,
            dst_ref=dst,
            send_sem=zsend_sem.at[i],
            recv_sem=zrecv_sem.at[i],
            device_id={"cp": partner},
            device_id_type=MESH,
        )

    def spread(q, owner, block):
        q = q.astype(F32) * SCALE
        high = q.astype(BF16)
        qx[owner, block, :, 0:WIDTH] = high
        qx[owner, block, :, WIDTH : 2 * WIDTH] = (q - high.astype(F32)).astype(BF16)

    def numbers(slot):
        tile = kbuf[slot, TOK:KROWS, :].astype(F32)
        wide = [jnp.concatenate([tile[8 * h : 8 * h + 1]] * (ROWS // WIDTH), axis=1) for h in range(2)]
        return wide

    def score_stage(owner, pair, block, diagonal=False):
        q = qx[owner, block]
        for a in range(2):
            keys = kbuf[2 * pair + a, 0:TOK, :]
            s = lax.dot_general(
                jnp.concatenate([keys, keys], axis=1), q, (((1,), (1,)), ((), ())), preferred_element_type=F32
            )
            for h in range(2):
                sh = s[h * SPAN : (h + 1) * SPAN]
                if diagonal and a == 0 and h == block:
                    key_off = lax.broadcasted_iota(jnp.int32, (SPAN, SPAN), 0)
                    query_off = lax.broadcasted_iota(jnp.int32, (SPAN, SPAN), 1)
                    seen = jnp.where(key_off <= query_off, 0.0, -BIG).astype(F32)
                    sh = sh + jnp.concatenate([seen] * GROUP, axis=1)
                at = a * TOK + h * SPAN
                scores[block][at : at + SPAN, :] = sh
                top = jnp.max(sh.reshape(SPAN // 8, 8, ROWS), axis=0)
                peaks[block][2 * a + h : 2 * a + h + 1, :] = jnp.max(top, axis=0, keepdims=True)

    def value_stage(owner, pair, block, diagonal=False):
        own = numbers(owner * UNITS)[block]
        old = maxs[block][owner]
        new = old
        seen = []
        for a in range(2):
            for h, number in enumerate(numbers(2 * pair + a)):
                visible = number <= own if diagonal and a == 0 else number < own
                seen.append(visible)
                row = 2 * a + h
                new = jnp.maximum(new, jnp.where(visible, peaks[block][row : row + 1, :], -BIG))
        maxs[block][owner] = new
        fade = jnp.exp2(old - new)
        total = sums[block][owner] * fade
        weights = []
        for i in range(4):
            shift = jnp.where(seen[i], new, BIG)
            p = jnp.exp2(scores[block][i * SPAN : (i + 1) * SPAN, :] - shift)
            total = total + jnp.sum(p.reshape(SPAN // 8, 8, ROWS), axis=0)
            weights.append(p.astype(BF16))
        values = jnp.concatenate([vbuf[2 * pair], vbuf[2 * pair + 1]], axis=1)
        product = jnp.dot(values, jnp.concatenate(weights, axis=0), preferred_element_type=F32)
        accs[block][owner] = accs[block][owner] * fade + product
        sums[block][owner] = total

    def diagonal_step(owner):
        for block in range(2):
            score_stage(owner, owner * (UNITS // 2), block, True)
        for block in range(2):
            value_stage(owner, owner * (UNITS // 2), block, True)

    def finish(owner, block):
        total = jnp.sum(sums[block][owner], axis=0, keepdims=True)
        return (accs[block][owner] / total).T.astype(BF16)

    barrier = pltpu.get_barrier_semaphore()
    neighbours = [device(0, 1), device(0, -1), device(1, 1), device(1, -1), partner]
    for n in neighbours:
        pl.semaphore_signal(barrier, inc=1, device_id={"cp": n}, device_id_type=MESH)
    pl.semaphore_wait(barrier, len(neighbours))

    forward(0, 0)
    for i in range(3):
        z_copy(i).start()
    kbuf[0] = k_ref[z]
    vbuf[0] = v_ref[z]
    for block in range(2):
        spread(q_ref[z, block], 0, block)
        accs[block][...] = jnp.zeros_like(accs[block])
        sums[block][...] = jnp.zeros_like(sums[block])
        maxs[block][...] = jnp.full(maxs[block].shape, -BIG, F32)
    arrive(0, 1)
    diagonal_step(0)
    arrive(0, 2)
    arrive(0, 3)

    half = UNITS // 2
    last = 4 * half - 3

    def place_of(t):
        owner = jnp.where((t >= half - 1) & (t < 3 * half - 2), 1, 0)
        pair = jnp.where(
            t < half - 1,
            t + 1,
            jnp.where(t < 2 * half - 1, t - (half - 1), jnp.where(t < 3 * half - 2, t - (half - 2), t - (2 * half - 2))),
        )
        return owner, pair

    def step(t, carry):
        for k in range(6):

            @pl.when(t == k)
            def _(k=k):
                arrive(0, 2 * k + 4)
                arrive(0, 2 * k + 5)
                if k == 3:
                    z_copy(0).wait_recv()
                    z_copy(1).wait_recv()
                    forward(1, 0)

        @pl.when(t == 6)
        def _():
            arrive(1, 1)
            z_copy(2).wait_recv()
            for block in range(2):
                spread(qz[block], 1, block)
            diagonal_step(1)
            score_stage(0, half - 1, 0)

        for k in range(7):

            @pl.when(t == half - 1 + k)
            def _(k=k):
                arrive(1, 2 * k + 2)
                arrive(1, 2 * k + 3)

        @pl.when(t == 3 * half - 2)
        def _():
            for block in range(2):
                oz[block] = finish(1, block)
            z_copy(3).start()

        owner, pair = place_of(t)
        owner2, pair2 = place_of(jnp.minimum(t + 1, last))
        score_stage(owner, pair, 1)
        value_stage(owner, pair, 0)
        score_stage(owner2, pair2, 0)
        value_stage(owner, pair, 1)
        return carry

    score_stage(0, 1, 0)
    lax.fori_loop(0, last + 1, step, 0)
    for block in range(2):
        o_ref[z, block] = finish(0, block)
    z_copy(3).wait_recv()
    for i in range(4):
        z_copy(i).wait_send()
    for wave in range(2):
        for n in range(UNITS):
            for kind in range(2):
                sends = forwards(kind, ORDER[n])
                for k in range(len(sends)):
                    send_copy(wave, kind, n, k, sends).wait_send()


def attend(q, k, v):
    scratch = [
        pltpu.VMEM((2 * UNITS, KROWS, WIDTH), BF16),
        pltpu.VMEM((2 * UNITS, WIDTH, TOK), BF16),
        pltpu.VMEM((2, 2, ROWS, 2 * WIDTH), BF16),
        pltpu.VMEM((2, ROWS, WIDTH), BF16),
        pltpu.VMEM((2, ROWS, WIDTH), BF16),
    ]
    for shape in [(2, WIDTH, ROWS)] * 2 + [(2, 1, ROWS)] * 2 + [(2, 8, ROWS)] * 2 + [(2 * TOK, ROWS)] * 2 + [(8, ROWS)] * 2:
        scratch.append(pltpu.VMEM(shape, F32))
    scratch += [
        pltpu.SemaphoreType.DMA((2, 2, N_SENDS)),
        pltpu.SemaphoreType.DMA((2, 2, UNITS, 2)),
        pltpu.SemaphoreType.DMA((4,)),
        pltpu.SemaphoreType.DMA((4,)),
    ]
    return pl.pallas_call(
        kernel,
        out_shape=jax.ShapeDtypeStruct((2, 2, ROWS, WIDTH), BF16),
        in_specs=[pl.BlockSpec(memory_space=pltpu.VMEM)] * 3,
        out_specs=pl.BlockSpec(memory_space=pltpu.VMEM),
        scratch_shapes=scratch,
        compiler_params=pltpu.CompilerParams(collective_id=0, has_side_effects=True, vmem_limit_bytes=56 << 20),
    )(q, k, v)


def body(queries, keys, values, positions):
    q = queries.reshape(2, SPAN, 2, GROUP, WIDTH).transpose(2, 0, 3, 1, 4).reshape(2, 2, ROWS, WIDTH)
    numbers = jnp.repeat(jnp.stack([positions[0], positions[SPAN]]) // SPAN, 8).astype(BF16)
    numbers = jnp.broadcast_to(numbers[None, :, None], (2, 16, WIDTH))
    k = jnp.concatenate([keys.transpose(1, 0, 2), numbers], axis=1)
    v = values.transpose(1, 2, 0)
    out = attend(q, k, v).reshape(2, 2, GROUP, SPAN, WIDTH)
    return out.transpose(1, 3, 0, 2, 4).reshape(TOK, 2 * GROUP, WIDTH)


def solution(mesh):
    return jax.shard_map(
        body,
        mesh=mesh,
        in_specs=(P("cp", "tp", None), P("cp", "tp", None), P("cp", "tp", None), P("cp")),
        out_specs=P("cp", "tp", None),
        check_vma=False,
    )
```

```python
import jax
import jax.numpy as jnp
from jax import lax
from jax.experimental import pallas as pl
from jax.experimental.pallas import tpu as pltpu
from jax.sharding import PartitionSpec as P

LOGICAL = pl.DeviceIdType.LOGICAL
F32 = jnp.float32
BF16 = jnp.bfloat16

SPAN = 192
TOK = 2 * SPAN
GROUP = 4
WIDTH = 128
ROWS = GROUP * SPAN
KROWS = TOK + 16
UROWS = KROWS + TOK
BIG = 1e30
SCALE = WIDTH**-0.5 * 1.4426950408889634

ORDER = [
    (0, 0),
    (-1, 0), (1, 0), (0, -1), (0, 1),
    (2, 0), (0, 2),
    (-1, -1), (1, 1), (-1, 1), (1, -1),
    (2, -1), (-1, 2), (2, 1), (1, 2),
    (2, 2),
]
UNITS = len(ORDER)
PAIRS = [[(0, 0), (1, 0)]]
for _wave in range(2):
    for _unit in range(1, 15, 2):
        PAIRS.append([(_wave, _unit), (_wave, _unit + 1)])
PAIRS.append([(0, 15), (1, 15)])
SLOT = {unit: 2 * r + a for r, pair in enumerate(PAIRS) for a, unit in enumerate(pair)}

RUNS = [(0, 1, 3), (1, 1, 3), (0, 4, 2), (1, 4, 2), (0, 6, 2), (1, 6, 2), (1, 8, 8), (0, 8, 8)]
STEPS = sum(run[2] for run in RUNS)
SERVICE = {
    1: [(0, 5), (0, 6)],
    4: [(0, 7), (0, 8), (0, 9), (0, 10)],
    7: [(0, 11), (0, 12), (0, 13), (0, 14)],
    9: [(0, 15)],
    10: [(1, 1), (1, 2), (1, 3), (1, 4)],
    12: [(1, 5), (1, 6)],
    15: [(1, 7), (1, 8), (1, 9), (1, 10)],
    18: [(1, 11), (1, 12), (1, 13), (1, 14)],
    20: [(1, 15)],
}
QUERIES_AT = 2
KEYS_AT = 5
DIAGONAL_AT = 6
OUTPUT_AT = 22


def wrap(d):
    return (d + 1) % 4 - 1


def forwards(wave, kind, n):
    place = ORDER[n]
    first, second = (0, 1) if kind == 0 else (1, 0)
    sends = []

    def send(axis, direction):
        there = list(place)
        there[axis] = wrap(there[axis] - direction)
        sends.append((axis, direction, ORDER.index(tuple(there))))

    around = 1 if wave == 0 else -1
    if place[second] == 0:
        if place[first] == 0:
            send(first, 1)
            send(first, -1)
        elif place[first] == -around:
            send(first, around)
        send(second, 1)
        send(second, -1)
    else:
        way = 1 if place[first] in (0, around) else -1
        if place[second] == -way:
            send(second, way)
    return sends


def kernel(
    q_ref, k_ref, v_ref, p_ref, o_ref,
    buf, kvz, qx, qs, qz, oz, qf, kf, vf, ids,
    acc0, acc1, m0, m1, l0, l1, s0, s1, c0, c1,
    send_sem, recv_sem, zsend_sem, zrecv_sem,
):
    accs, maxs, sums = (acc0, acc1), (m0, m1), (l0, l1)
    scores, peaks = (s0, s1), (c0, c1)
    cp = lax.axis_index("cp")
    y, x, z = cp // 8, (cp // 2) % 4, cp % 2
    other = 1 - z

    base = lax.axis_index("tp") * 32 + z
    device = {
        (0, 1): base + (y * 4 + (x + 1) % 4) * 2,
        (0, -1): base + (y * 4 + (x + 3) % 4) * 2,
        (1, 1): base + (((y + 1) % 4) * 4 + x) * 2,
        (1, -1): base + (((y + 3) % 4) * 4 + x) * 2,
    }
    partner = base + (y * 4 + x) * 2 + other - z

    def rows(kind):
        return slice(0, KROWS) if kind == 0 else slice(KROWS, UROWS)

    def copy(src, dst, ssem, rsem, target):
        return pltpu.make_async_remote_copy(
            src_ref=src,
            dst_ref=dst,
            send_sem=ssem,
            recv_sem=rsem,
            device_id=target,
            device_id_type=LOGICAL,
        )

    def forward(wave, n):
        for kind in range(2):
            for axis, direction, there in forwards(wave, kind, n):
                copy(
                    buf.at[SLOT[(wave, n)], rows(kind)],
                    buf.at[SLOT[(wave, there)], rows(kind)],
                    send_sem.at[wave],
                    recv_sem.at[wave, there],
                    device[axis, direction],
                ).start()

    def arrive(wave, n):
        here = buf.at[SLOT[(wave, n)]]
        copy(here, here, send_sem.at[wave], recv_sem.at[wave, n], partner).wait_recv()
        forward(wave, n)

    def z_copy(i):
        src, dst = (
            (qs, qz),
            (kvz, buf.at[SLOT[(1, 0)]]),
            (oz, o_ref.at[z]),
        )[i]
        return copy(src, dst, zsend_sem.at[i], zrecv_sem.at[i], partner)

    def spread(q, owner, block, h):
        q = q * SCALE
        high = q.astype(BF16)
        rows = slice(h * SPAN, (h + 1) * SPAN)
        qx[owner, block, rows, 0:WIDTH] = high
        qx[owner, block, rows, WIDTH : 2 * WIDTH] = (q - high.astype(F32)).astype(BF16)

    def head(owner_z, block, h):
        return qf[pl.ds(block * SPAN * 2 * GROUP + GROUP * owner_z + h, SPAN, stride=2 * GROUP), :]

    def spread_keys():
        kf[...] = k_ref[...].astype(F32)
        vf[...] = v_ref[...].astype(F32)
        blocks = [jnp.full((8, WIDTH), p_ref[b * SPAN] // SPAN, jnp.int32).astype(F32) for b in range(2)]
        for b in range(2):
            ids[0, b] = blocks[b]
            qs[b, ROWS:, :] = jnp.concatenate([blocks[b]] * 2, axis=0).astype(BF16)
        for served, put in ((z, buf.at[0]), (other, kvz)):
            put[0:TOK, :] = kf[pl.ds(served, TOK, stride=2), :].astype(BF16)
            put[TOK:KROWS, :] = jnp.concatenate(blocks, axis=0).astype(BF16)
            for c in range(TOK // WIDTH):
                v = vf[pl.ds(2 * WIDTH * c + served, WIDTH, stride=2), :]
                put[KROWS + c * WIDTH : KROWS + (c + 1) * WIDTH, :] = v.T.astype(BF16)

    def wide(tile):
        return jnp.concatenate([tile[0:1]] * (ROWS // WIDTH), axis=1)

    def numbers(slot):
        tile = buf[slot, TOK:KROWS, :].astype(F32)
        return [wide(tile[8 * h : 8 * h + 8]) for h in range(2)]

    def score_stage(owner, slots, block, diagonal=None):
        q = qx[owner, block]
        for a, slot in enumerate(slots):
            keys = buf[slot, 0:TOK, :]
            s = lax.dot_general(
                jnp.concatenate([keys, keys], axis=1), q, (((1,), (1,)), ((), ())), preferred_element_type=F32
            )
            for h in range(2):
                sh = s[h * SPAN : (h + 1) * SPAN]
                if diagonal == a and h == block:
                    key_off = lax.broadcasted_iota(jnp.int32, (SPAN, SPAN), 0)
                    query_off = lax.broadcasted_iota(jnp.int32, (SPAN, SPAN), 1)
                    seen = jnp.where(key_off <= query_off, 0.0, -BIG).astype(F32)
                    sh = sh + jnp.concatenate([seen] * GROUP, axis=1)
                at = a * TOK + h * SPAN
                scores[block][at : at + SPAN, :] = sh
                top = jnp.max(sh.reshape(SPAN // 8, 8, ROWS), axis=0)
                peaks[block][2 * a + h : 2 * a + h + 1, :] = jnp.max(top, axis=0, keepdims=True)

    def value_stage(owner, slots, block, diagonal=None):
        own = wide(ids[owner, block])
        old = maxs[block][owner]
        new = old
        seen = []
        for a, slot in enumerate(slots):
            for h, number in enumerate(numbers(slot)):
                visible = number <= own if diagonal == a else number < own
                seen.append(visible)
                row = 2 * a + h
                new = jnp.maximum(new, jnp.where(visible, peaks[block][row : row + 1, :], -BIG))
        maxs[block][owner] = new
        fade = jnp.exp2(old - new)
        total = sums[block][owner] * fade
        weights = []
        for i, visible in enumerate(seen):
            shift = jnp.where(visible, new, BIG)
            p = jnp.exp2(scores[block][i * SPAN : (i + 1) * SPAN, :] - shift)
            total = total + jnp.sum(p.reshape(SPAN // 8, 8, ROWS), axis=0)
            weights.append(p.astype(BF16))
        values = jnp.concatenate(
            [buf[slot, KROWS + c * WIDTH : KROWS + (c + 1) * WIDTH, :] for slot in slots for c in range(TOK // WIDTH)],
            axis=1,
        )
        product = jnp.dot(values, jnp.concatenate(weights, axis=0), preferred_element_type=F32)
        accs[block][owner] = accs[block][owner] * fade + product
        sums[block][owner] = total

    def single_step(owner, slots, diagonal):
        for block in range(2):
            score_stage(owner, slots, block, diagonal)
        for block in range(2):
            value_stage(owner, slots, block, diagonal)

    def finish(owner, block):
        total = jnp.sum(sums[block][owner], axis=0, keepdims=True)
        return (accs[block][owner] / total).T.astype(BF16)

    barrier = pltpu.get_barrier_semaphore()
    neighbours = [*device.values(), partner]
    for n in neighbours:
        pl.semaphore_signal(barrier, inc=1, device_id=n, device_id_type=LOGICAL)
    spread_keys()
    pl.semaphore_wait(barrier, len(neighbours))

    forward(0, 0)
    qf[...] = q_ref[...].astype(F32)
    for block in range(2):
        for h in range(GROUP):
            qs[block, h * SPAN : (h + 1) * SPAN, :] = head(other, block, h).astype(BF16)
    z_copy(0).start()
    z_copy(1).start()
    for block in range(2):
        for h in range(GROUP):
            spread(head(z, block, h), 0, block, h)
        accs[block][...] = jnp.zeros_like(accs[block])
        sums[block][...] = jnp.zeros_like(sums[block])
        maxs[block][...] = jnp.full(maxs[block].shape, -BIG, F32)
    single_step(0, [0], 0)
    for n in range(1, 5):
        arrive(0, n)

    def place_of(t):
        owner, pair, begin = jnp.int32(0), t, 0
        for own, first, pairs in RUNS:
            owner = jnp.where(t >= begin, own, owner)
            pair = jnp.where(t >= begin, t - begin + first, pair)
            begin += pairs
        return owner, [2 * pair, 2 * pair + 1]

    def queries_come():
        z_copy(0).wait_recv()
        for block in range(2):
            ids[1, block] = qz[block, ROWS:, :].astype(F32)[0:8]
            for h in range(GROUP):
                spread(qz[block, h * SPAN : (h + 1) * SPAN, :].astype(F32), 1, block, h)

    def keys_come():
        z_copy(1).wait_recv()
        forward(1, 0)

    def diagonal_meets():
        single_step(0, [1], None)
        single_step(1, [0, 1], 1)
        owner, slots = place_of(jnp.int32(DIAGONAL_AT))
        score_stage(owner, slots, 0)

    def outputs_go():
        for block in range(2):
            oz[block] = finish(1, block)
        z_copy(2).start()

    events = {at: [lambda unit=unit: arrive(*unit) for unit in units] for at, units in SERVICE.items()}
    for at, event in (
        (QUERIES_AT, queries_come),
        (KEYS_AT, keys_come),
        (DIAGONAL_AT, diagonal_meets),
        (OUTPUT_AT, outputs_go),
    ):
        events.setdefault(at, []).append(event)
    starts = sorted(events)

    def step(t, carry):
        owner, slots = place_of(t)
        owner2, slots2 = place_of(jnp.minimum(t + 1, STEPS - 1))
        score_stage(owner, slots, 1)
        value_stage(owner, slots, 0)
        score_stage(owner2, slots2, 0)
        value_stage(owner, slots, 1)
        return carry

    def stretch(e, carry):
        begin, end = jnp.int32(0), jnp.int32(STEPS)
        for i, at in enumerate(starts):
            begin = jnp.where(e == i + 1, at, begin)
            end = jnp.where(e == i, at, end)

            @pl.when(e == i + 1)
            def _(at=at):
                for event in events[at]:
                    event()

        return lax.fori_loop(begin, end, step, carry)

    score_stage(0, [2, 3], 0)
    lax.fori_loop(0, len(starts) + 1, stretch, 0)
    for block in range(2):
        o_ref[z, block] = finish(0, block)
    z_copy(2).wait_recv()
    for i in range(3):
        z_copy(i).wait_send()
    for wave in range(2):
        sent = buf.at[0 : UNITS - 1]
        copy(sent, sent, send_sem.at[wave], recv_sem.at[wave, 0], partner).wait_send()


def attend(q, k, v, positions):
    scratch = [
        pltpu.VMEM((2 * UNITS, UROWS, WIDTH), BF16),
        pltpu.VMEM((UROWS, WIDTH), BF16),
        pltpu.VMEM((2, 2, ROWS, 2 * WIDTH), BF16),
        pltpu.VMEM((2, ROWS + 16, WIDTH), BF16),
        pltpu.VMEM((2, ROWS + 16, WIDTH), BF16),
        pltpu.VMEM((2, ROWS, WIDTH), BF16),
        pltpu.VMEM(q.shape, F32),
        pltpu.VMEM(k.shape, F32),
        pltpu.VMEM(v.shape, F32),
        pltpu.VMEM((2, 2, 8, WIDTH), F32),
    ]
    for shape in [(2, WIDTH, ROWS)] * 2 + [(2, 1, ROWS)] * 2 + [(2, 8, ROWS)] * 2 + [(2 * TOK, ROWS)] * 2 + [(8, ROWS)] * 2:
        scratch.append(pltpu.VMEM(shape, F32))
    scratch += [
        pltpu.SemaphoreType.DMA((2,)),
        pltpu.SemaphoreType.DMA((2, UNITS)),
        pltpu.SemaphoreType.DMA((3,)),
        pltpu.SemaphoreType.DMA((3,)),
    ]
    return pl.pallas_call(
        kernel,
        out_shape=jax.ShapeDtypeStruct((2, 2, ROWS, WIDTH), BF16),
        in_specs=[pl.BlockSpec(memory_space=pltpu.VMEM)] * 3 + [pl.BlockSpec(memory_space=pltpu.SMEM)],
        out_specs=pl.BlockSpec(memory_space=pltpu.VMEM),
        scratch_shapes=scratch,
        compiler_params=pltpu.CompilerParams(collective_id=0, has_side_effects=True, vmem_limit_bytes=56 << 20),
    )(q, k, v, positions)


def body(queries, keys, values, positions):
    rows = [a.reshape(-1, WIDTH) for a in (queries, keys, values)]
    out = attend(*rows, positions).reshape(2, 2, GROUP, SPAN, WIDTH)
    return out.transpose(1, 3, 0, 2, 4).reshape(TOK, 2 * GROUP, WIDTH)


def solution(mesh):
    return jax.shard_map(
        body,
        mesh=mesh,
        in_specs=(P("cp", "tp", None), P("cp", "tp", None), P("cp", "tp", None), P("cp")),
        out_specs=P("cp", "tp", None),
        check_vma=False,
    )
```

```python
import jax
import jax.numpy as jnp
from jax import lax
from jax.experimental import pallas as pl
from jax.experimental.pallas import tpu as pltpu
from jax.sharding import PartitionSpec as P

LOGICAL = pl.DeviceIdType.LOGICAL
F32 = jnp.float32
BF16 = jnp.bfloat16

SPAN = 192
TOK = 2 * SPAN
GROUP = 4
WIDTH = 128
ROWS = GROUP * SPAN
KROWS = TOK + 16
UROWS = KROWS + TOK
BIG = 1e30
SCALE = WIDTH**-0.5 * 1.4426950408889634

ORDER = [
    (0, 0),
    (-1, 0), (1, 0), (0, -1), (0, 1),
    (2, 0), (0, 2),
    (-1, -1), (1, 1), (-1, 1), (1, -1),
    (2, -1), (-1, 2), (2, 1), (1, 2),
    (2, 2),
]
UNITS = len(ORDER)
PAIRS = [[(0, 0), (1, 0)]]
for _wave in range(2):
    for _unit in range(1, 15, 2):
        PAIRS.append([(_wave, _unit), (_wave, _unit + 1)])
PAIRS.append([(0, 15), (1, 15)])
SLOT = {unit: 2 * r + a for r, pair in enumerate(PAIRS) for a, unit in enumerate(pair)}

RUNS = [
    (0, 1, 2), (1, 1, 2), (0, 3, 1), (1, 3, 1), (0, 4, 2), (1, 4, 2), (0, 6, 2), (1, 6, 2),
    (1, 8, 4), (0, 8, 1), (1, 12, 4), (0, 9, 7),
]
STEPS = sum(run[2] for run in RUNS)
SERVICE = {
    3: [(0, 5), (0, 6)],
    4: [(0, 7), (0, 8), (0, 9), (0, 10)],
    8: [(1, 1), (1, 2), (1, 3), (1, 4)],
    9: [(0, 11), (0, 12), (0, 13), (0, 14)],
    11: [(0, 15)],
    12: [(1, 5), (1, 6)],
    14: [(1, 7), (1, 8), (1, 9), (1, 10)],
    18: [(1, 11), (1, 12), (1, 13), (1, 14)],
    20: [(1, 15)],
}
QUERIES_AT = 1
KEYS_AT = 4
DIAGONAL_AT = 6
OUTPUT_AT = 23


def wrap(d):
    return (d + 1) % 4 - 1


def forwards(wave, kind, n):
    place = ORDER[n]
    first, second = (0, 1) if kind == 0 else (1, 0)
    sends = []

    def send(axis, direction):
        there = list(place)
        there[axis] = wrap(there[axis] - direction)
        sends.append((axis, direction, ORDER.index(tuple(there))))

    around = 1 if wave == 0 else -1
    if place[second] == 0:
        if place[first] == 0:
            send(first, 1)
            send(first, -1)
        elif place[first] == -around:
            send(first, around)
        send(second, 1)
        send(second, -1)
    else:
        way = -1 if place[first] in (0, around) else 1
        if place[second] == -way:
            send(second, way)
    return sends


def kernel(
    q_ref, k_ref, v_ref, p_ref, o_ref,
    buf, kvz, qx, qs, qz, oz, qf, kf, vf, ids,
    acc0, acc1, m0, m1, l0, l1, s0, s1, c0, c1,
    send_sem, recv_sem, zsend_sem, zrecv_sem,
):
    accs, maxs, sums = (acc0, acc1), (m0, m1), (l0, l1)
    scores, peaks = (s0, s1), (c0, c1)
    cp = lax.axis_index("cp")
    y, x, z = cp // 8, (cp // 2) % 4, cp % 2
    other = 1 - z

    base = lax.axis_index("tp") * 32 + z
    device = {
        (0, 1): base + (y * 4 + (x + 1) % 4) * 2,
        (0, -1): base + (y * 4 + (x + 3) % 4) * 2,
        (1, 1): base + (((y + 1) % 4) * 4 + x) * 2,
        (1, -1): base + (((y + 3) % 4) * 4 + x) * 2,
    }
    partner = base + (y * 4 + x) * 2 + other - z

    def rows(kind):
        return slice(0, KROWS) if kind == 0 else slice(KROWS, UROWS)

    def copy(src, dst, ssem, rsem, target):
        return pltpu.make_async_remote_copy(
            src_ref=src,
            dst_ref=dst,
            send_sem=ssem,
            recv_sem=rsem,
            device_id=target,
            device_id_type=LOGICAL,
        )

    def forward(units):
        sends = [(*send, kind, wave, n) for wave, n in units for kind in range(2) for send in forwards(wave, kind, n)]
        for axis, direction, there, kind, wave, n in sorted(sends, key=lambda send: send[2]):
            copy(
                buf.at[SLOT[(wave, n)], rows(kind)],
                buf.at[SLOT[(wave, there)], rows(kind)],
                send_sem.at[wave],
                recv_sem.at[wave, there],
                device[axis, direction],
            ).start()

    def arrive(units):
        for wave, n in units:
            here = buf.at[SLOT[(wave, n)]]
            copy(here, here, send_sem.at[wave], recv_sem.at[wave, n], partner).wait_recv()
        forward(units)

    def z_copy(i):
        src, dst = (
            (qs, qz),
            (kvz, buf.at[SLOT[(1, 0)]]),
            (oz, o_ref.at[z]),
        )[i]
        return copy(src, dst, zsend_sem.at[i], zrecv_sem.at[i], partner)

    def spread(q, owner, block, h):
        q = q * SCALE
        high = q.astype(BF16)
        rows = slice(h * SPAN, (h + 1) * SPAN)
        qx[owner, block, rows, 0:WIDTH] = high
        qx[owner, block, rows, WIDTH : 2 * WIDTH] = (q - high.astype(F32)).astype(BF16)

    def head(owner_z, block, h):
        return qf[pl.ds(block * SPAN * 2 * GROUP + GROUP * owner_z + h, SPAN, stride=2 * GROUP), :]

    def spread_keys():
        kf[...] = k_ref[...].astype(F32)
        vf[...] = v_ref[...].astype(F32)
        blocks = [jnp.full((8, WIDTH), p_ref[b * SPAN] // SPAN, jnp.int32).astype(F32) for b in range(2)]
        for b in range(2):
            ids[0, b] = blocks[b]
            qs[b, ROWS:, :] = jnp.concatenate([blocks[b]] * 2, axis=0).astype(BF16)
        for served, put in ((z, buf.at[0]), (other, kvz)):
            put[0:TOK, :] = kf[pl.ds(served, TOK, stride=2), :].astype(BF16)
            put[TOK:KROWS, :] = jnp.concatenate(blocks, axis=0).astype(BF16)
            for c in range(TOK // WIDTH):
                v = vf[pl.ds(2 * WIDTH * c + served, WIDTH, stride=2), :]
                put[KROWS + c * WIDTH : KROWS + (c + 1) * WIDTH, :] = v.T.astype(BF16)

    def wide(tile):
        return jnp.concatenate([tile[0:1]] * (ROWS // WIDTH), axis=1)

    def numbers(slot):
        tile = buf[slot, TOK:KROWS, :].astype(F32)
        return [wide(tile[8 * h : 8 * h + 8]) for h in range(2)]

    def score_stage(owner, slots, block, diagonal=None):
        q = qx[owner, block]
        for a, slot in enumerate(slots):
            keys = buf[slot, 0:TOK, :]
            s = lax.dot_general(
                jnp.concatenate([keys, keys], axis=1), q, (((1,), (1,)), ((), ())), preferred_element_type=F32
            )
            for h in range(2):
                sh = s[h * SPAN : (h + 1) * SPAN]
                if diagonal == a and h == block:
                    key_off = lax.broadcasted_iota(jnp.int32, (SPAN, SPAN), 0)
                    query_off = lax.broadcasted_iota(jnp.int32, (SPAN, SPAN), 1)
                    seen = jnp.where(key_off <= query_off, 0.0, -BIG).astype(F32)
                    sh = sh + jnp.concatenate([seen] * GROUP, axis=1)
                at = a * TOK + h * SPAN
                scores[block][at : at + SPAN, :] = sh
                top = jnp.max(sh.reshape(SPAN // 8, 8, ROWS), axis=0)
                peaks[block][2 * a + h : 2 * a + h + 1, :] = jnp.max(top, axis=0, keepdims=True)

    def value_stage(owner, slots, block, diagonal=None):
        own = wide(ids[owner, block])
        old = maxs[block][owner]
        new = old
        seen = []
        for a, slot in enumerate(slots):
            for h, number in enumerate(numbers(slot)):
                visible = number <= own if diagonal == a else number < own
                seen.append(visible)
                row = 2 * a + h
                new = jnp.maximum(new, jnp.where(visible, peaks[block][row : row + 1, :], -BIG))
        maxs[block][owner] = new
        fade = jnp.exp2(old - new)
        total = sums[block][owner] * fade
        weights = []
        for i, visible in enumerate(seen):
            shift = jnp.where(visible, new, BIG)
            p = jnp.exp2(scores[block][i * SPAN : (i + 1) * SPAN, :] - shift)
            total = total + jnp.sum(p.reshape(SPAN // 8, 8, ROWS), axis=0)
            weights.append(p.astype(BF16))
        values = jnp.concatenate(
            [buf[slot, KROWS + c * WIDTH : KROWS + (c + 1) * WIDTH, :] for slot in slots for c in range(TOK // WIDTH)],
            axis=1,
        )
        product = jnp.dot(values, jnp.concatenate(weights, axis=0), preferred_element_type=F32)
        accs[block][owner] = accs[block][owner] * fade + product
        sums[block][owner] = total

    def single_step(owner, slots, diagonal):
        for block in range(2):
            score_stage(owner, slots, block, diagonal)
        for block in range(2):
            value_stage(owner, slots, block, diagonal)

    def finish(owner, block):
        total = jnp.sum(sums[block][owner], axis=0, keepdims=True)
        return (accs[block][owner] / total).T.astype(BF16)

    barrier = pltpu.get_barrier_semaphore()
    neighbours = [*device.values(), partner]
    for n in neighbours:
        pl.semaphore_signal(barrier, inc=1, device_id=n, device_id_type=LOGICAL)
    spread_keys()
    pl.semaphore_wait(barrier, len(neighbours))

    forward([(0, 0)])
    qf[...] = q_ref[...].astype(F32)
    for block in range(2):
        for h in range(GROUP):
            qs[block, h * SPAN : (h + 1) * SPAN, :] = head(other, block, h).astype(BF16)
    z_copy(0).start()
    z_copy(1).start()
    for block in range(2):
        for h in range(GROUP):
            spread(head(z, block, h), 0, block, h)
        accs[block][...] = jnp.zeros_like(accs[block])
        sums[block][...] = jnp.zeros_like(sums[block])
        maxs[block][...] = jnp.full(maxs[block].shape, -BIG, F32)
    single_step(0, [0], 0)
    arrive([(0, n) for n in range(1, 5)])

    def place_of(t):
        owner, pair, begin = jnp.int32(0), t, 0
        for own, first, pairs in RUNS:
            owner = jnp.where(t >= begin, own, owner)
            pair = jnp.where(t >= begin, t - begin + first, pair)
            begin += pairs
        return owner, [2 * pair, 2 * pair + 1]

    def queries_come():
        z_copy(0).wait_recv()
        for block in range(2):
            ids[1, block] = qz[block, ROWS:, :].astype(F32)[0:8]
            for h in range(GROUP):
                spread(qz[block, h * SPAN : (h + 1) * SPAN, :].astype(F32), 1, block, h)

    def keys_come():
        z_copy(1).wait_recv()
        forward([(1, 0)])

    def diagonal_meets():
        single_step(0, [1], None)
        single_step(1, [0, 1], 1)
        owner, slots = place_of(jnp.int32(DIAGONAL_AT))
        score_stage(owner, slots, 0)

    def outputs_go():
        for block in range(2):
            oz[block] = finish(1, block)
        z_copy(2).start()

    events = {at: [lambda units=units: arrive(units)] for at, units in SERVICE.items()}
    for at, event in (
        (QUERIES_AT, queries_come),
        (KEYS_AT, keys_come),
        (DIAGONAL_AT, diagonal_meets),
        (OUTPUT_AT, outputs_go),
    ):
        events.setdefault(at, []).insert(0, event)
    starts = sorted(events)

    def step(t, carry):
        owner, slots = place_of(t)
        owner2, slots2 = place_of(jnp.minimum(t + 1, STEPS - 1))
        score_stage(owner, slots, 1)
        value_stage(owner, slots, 0)
        score_stage(owner2, slots2, 0)
        value_stage(owner, slots, 1)
        return carry

    def stretch(e, carry):
        begin, end = jnp.int32(0), jnp.int32(STEPS)
        for i, at in enumerate(starts):
            begin = jnp.where(e == i + 1, at, begin)
            end = jnp.where(e == i, at, end)

            @pl.when(e == i + 1)
            def _(at=at):
                for event in events[at]:
                    event()

        return lax.fori_loop(begin, end, step, carry)

    score_stage(0, [2, 3], 0)
    lax.fori_loop(0, len(starts) + 1, stretch, 0)
    for block in range(2):
        o_ref[z, block] = finish(0, block)
    z_copy(2).wait_recv()
    for i in range(3):
        z_copy(i).wait_send()
    for wave in range(2):
        sent = buf.at[0 : UNITS - 1]
        copy(sent, sent, send_sem.at[wave], recv_sem.at[wave, 0], partner).wait_send()


def attend(q, k, v, positions):
    scratch = [
        pltpu.VMEM((2 * UNITS, UROWS, WIDTH), BF16),
        pltpu.VMEM((UROWS, WIDTH), BF16),
        pltpu.VMEM((2, 2, ROWS, 2 * WIDTH), BF16),
        pltpu.VMEM((2, ROWS + 16, WIDTH), BF16),
        pltpu.VMEM((2, ROWS + 16, WIDTH), BF16),
        pltpu.VMEM((2, ROWS, WIDTH), BF16),
        pltpu.VMEM(q.shape, F32),
        pltpu.VMEM(k.shape, F32),
        pltpu.VMEM(v.shape, F32),
        pltpu.VMEM((2, 2, 8, WIDTH), F32),
    ]
    for shape in [(2, WIDTH, ROWS)] * 2 + [(2, 1, ROWS)] * 2 + [(2, 8, ROWS)] * 2 + [(2 * TOK, ROWS)] * 2 + [(8, ROWS)] * 2:
        scratch.append(pltpu.VMEM(shape, F32))
    scratch += [
        pltpu.SemaphoreType.DMA((2,)),
        pltpu.SemaphoreType.DMA((2, UNITS)),
        pltpu.SemaphoreType.DMA((3,)),
        pltpu.SemaphoreType.DMA((3,)),
    ]
    return pl.pallas_call(
        kernel,
        out_shape=jax.ShapeDtypeStruct((2, 2, ROWS, WIDTH), BF16),
        in_specs=[pl.BlockSpec(memory_space=pltpu.VMEM)] * 3 + [pl.BlockSpec(memory_space=pltpu.SMEM)],
        out_specs=pl.BlockSpec(memory_space=pltpu.VMEM),
        scratch_shapes=scratch,
        compiler_params=pltpu.CompilerParams(collective_id=0, has_side_effects=True, vmem_limit_bytes=56 << 20),
    )(q, k, v, positions)


def body(queries, keys, values, positions):
    rows = [a.reshape(-1, WIDTH) for a in (queries, keys, values)]
    out = attend(*rows, positions).reshape(2, 2, GROUP, SPAN, WIDTH)
    return out.transpose(1, 3, 0, 2, 4).reshape(TOK, 2 * GROUP, WIDTH)


def solution(mesh):
    return jax.shard_map(
        body,
        mesh=mesh,
        in_specs=(P("cp", "tp", None), P("cp", "tp", None), P("cp", "tp", None), P("cp")),
        out_specs=P("cp", "tp", None),
        check_vma=False,
    )
```

```python
import jax
import jax.numpy as jnp
from jax import lax
from jax.experimental import pallas as pl
from jax.experimental.pallas import tpu as pltpu
from jax.sharding import PartitionSpec as P

LOGICAL = pl.DeviceIdType.LOGICAL
F32 = jnp.float32
BF16 = jnp.bfloat16

SPAN = 192
TOK = 2 * SPAN
GROUP = 4
WIDTH = 128
ROWS = GROUP * SPAN
KROWS = TOK + 16
UROWS = KROWS + TOK
BIG = 1e30
SCALE = WIDTH**-0.5 * 1.4426950408889634

ORDER = [
    (0, 0),
    (-1, 0), (1, 0), (0, -1), (0, 1),
    (2, 0), (0, 2),
    (-1, -1), (1, 1), (-1, 1), (1, -1),
    (2, -1), (-1, 2), (2, 1), (1, 2),
    (2, 2),
]
UNITS = len(ORDER)
PAIRS = [[(0, 0), (1, 0)]]
for _wave in range(2):
    for _unit in range(1, 15, 2):
        PAIRS.append([(_wave, _unit), (_wave, _unit + 1)])
PAIRS.append([(0, 15), (1, 15)])
SLOT = {unit: 2 * r + a for r, pair in enumerate(PAIRS) for a, unit in enumerate(pair)}

RUNS = [
    (0, 1, 2), (1, 1, 2), (0, 3, 1), (1, 3, 1), (0, 4, 2), (1, 4, 2), (0, 6, 2), (1, 6, 2),
    (1, 8, 4), (0, 8, 1), (1, 12, 4), (0, 9, 7),
]
STEPS = sum(run[2] for run in RUNS)
SERVICE = {
    3: [(0, 5), (0, 6)],
    4: [(0, 7), (0, 8), (0, 9), (0, 10)],
    7: [(1, 1), (1, 2), (1, 3), (1, 4)],
    8: [(0, 11), (0, 12), (0, 13), (0, 14)],
    11: [(0, 15), (1, 5), (1, 6)],
    13: [(1, 7), (1, 8), (1, 9), (1, 10)],
    17: [(1, 11), (1, 12), (1, 13), (1, 14)],
    20: [(1, 15)],
}
QUERIES_AT = 1
KEYS_AT = 4
DIAGONAL_AT = 6
OUTPUT_AT = 23


def wrap(d):
    return (d + 1) % 4 - 1


def forwards(wave, kind, n):
    place = ORDER[n]
    first, second = (0, 1) if kind == 0 else (1, 0)
    sends = []

    def send(axis, direction):
        there = list(place)
        there[axis] = wrap(there[axis] - direction)
        sends.append((axis, direction, ORDER.index(tuple(there))))

    around = 1 if wave == 0 else -1
    if place[second] == 0:
        if place[first] == 0:
            send(first, 1)
            send(first, -1)
        elif place[first] == -around:
            send(first, around)
        send(second, 1)
        send(second, -1)
    else:
        way = -1 if place[first] in (0, around) else 1
        if place[second] == -way:
            send(second, way)
    return sends


def kernel(
    q_ref, k_ref, v_ref, p_ref, o_ref,
    buf, kvz, qx, qs, qz, oz, qf, kf, vf, ids,
    acc0, acc1, m0, m1, l0, l1, s0, s1, c0, c1,
    send_sem, recv_sem, zsend_sem, zrecv_sem,
):
    accs, maxs, sums = (acc0, acc1), (m0, m1), (l0, l1)
    scores, peaks = (s0, s1), (c0, c1)
    cp = lax.axis_index("cp")
    y, x, z = cp // 8, (cp // 2) % 4, cp % 2
    other = 1 - z

    base = lax.axis_index("tp") * 32 + z
    device = {
        (0, 1): base + (y * 4 + (x + 1) % 4) * 2,
        (0, -1): base + (y * 4 + (x + 3) % 4) * 2,
        (1, 1): base + (((y + 1) % 4) * 4 + x) * 2,
        (1, -1): base + (((y + 3) % 4) * 4 + x) * 2,
    }
    partner = base + (y * 4 + x) * 2 + other - z

    def rows(kind):
        return slice(0, KROWS) if kind == 0 else slice(KROWS, UROWS)

    def copy(src, dst, ssem, rsem, target):
        return pltpu.make_async_remote_copy(
            src_ref=src,
            dst_ref=dst,
            send_sem=ssem,
            recv_sem=rsem,
            device_id=target,
            device_id_type=LOGICAL,
        )

    def forward(units):
        sends = [(*send, kind, wave, n) for wave, n in units for kind in range(2) for send in forwards(wave, kind, n)]
        for axis, direction, there, kind, wave, n in sorted(sends, key=lambda send: send[2]):
            copy(
                buf.at[SLOT[(wave, n)], rows(kind)],
                buf.at[SLOT[(wave, there)], rows(kind)],
                send_sem.at[wave],
                recv_sem.at[wave, there],
                device[axis, direction],
            ).start()

    def arrive(units):
        for wave, n in units:
            here = buf.at[SLOT[(wave, n)]]
            copy(here, here, send_sem.at[wave], recv_sem.at[wave, n], partner).wait_recv()
        forward(units)

    def z_copy(i):
        src, dst = (
            (qs.at[0], qz.at[0]),
            (qs.at[1], qz.at[1]),
            (kvz, buf.at[SLOT[(1, 0)]]),
            (oz, o_ref.at[z]),
        )[i]
        return copy(src, dst, zsend_sem.at[i], zrecv_sem.at[i], partner)

    def spread(q, owner, block, h):
        q = q * SCALE
        high = q.astype(BF16)
        rows = slice(h * SPAN, (h + 1) * SPAN)
        qx[owner, block, rows, 0:WIDTH] = high
        qx[owner, block, rows, WIDTH : 2 * WIDTH] = (q - high.astype(F32)).astype(BF16)

    def head(owner_z, block, h):
        return qf[pl.ds(block * SPAN * 2 * GROUP + GROUP * owner_z + h, SPAN, stride=2 * GROUP), :]

    def spread_keys():
        kf[...] = k_ref[...].astype(F32)
        vf[...] = v_ref[...].astype(F32)
        blocks = [jnp.full((8, WIDTH), p_ref[b * SPAN] // SPAN, jnp.int32).astype(F32) for b in range(2)]
        for b in range(2):
            ids[0, b] = blocks[b]
            qs[b, ROWS:, :] = jnp.concatenate([blocks[b]] * 2, axis=0).astype(BF16)
        for served, put in ((z, buf.at[0]), (other, kvz)):
            put[0:TOK, :] = kf[pl.ds(served, TOK, stride=2), :].astype(BF16)
            put[TOK:KROWS, :] = jnp.concatenate(blocks, axis=0).astype(BF16)
            for c in range(TOK // WIDTH):
                v = vf[pl.ds(2 * WIDTH * c + served, WIDTH, stride=2), :]
                put[KROWS + c * WIDTH : KROWS + (c + 1) * WIDTH, :] = v.T.astype(BF16)

    def wide(tile):
        return jnp.concatenate([tile[0:1]] * (ROWS // WIDTH), axis=1)

    def numbers(slot):
        tile = buf[slot, TOK:KROWS, :].astype(F32)
        return [wide(tile[8 * h : 8 * h + 8]) for h in range(2)]

    def score_stage(owner, slots, block, diagonal=None):
        q = qx[owner, block]
        for a, slot in enumerate(slots):
            keys = buf[slot, 0:TOK, :]
            s = lax.dot_general(
                jnp.concatenate([keys, keys], axis=1), q, (((1,), (1,)), ((), ())), preferred_element_type=F32
            )
            for h in range(2):
                sh = s[h * SPAN : (h + 1) * SPAN]
                if diagonal == a and h == block:
                    key_off = lax.broadcasted_iota(jnp.int32, (SPAN, SPAN), 0)
                    query_off = lax.broadcasted_iota(jnp.int32, (SPAN, SPAN), 1)
                    seen = jnp.where(key_off <= query_off, 0.0, -BIG).astype(F32)
                    sh = sh + jnp.concatenate([seen] * GROUP, axis=1)
                at = a * TOK + h * SPAN
                scores[block][at : at + SPAN, :] = sh
                top = jnp.max(sh.reshape(SPAN // 8, 8, ROWS), axis=0)
                peaks[block][2 * a + h : 2 * a + h + 1, :] = jnp.max(top, axis=0, keepdims=True)

    def value_stage(owner, slots, block, diagonal=None):
        own = wide(ids[owner, block])
        old = maxs[block][owner]
        new = old
        seen = []
        for a, slot in enumerate(slots):
            for h, number in enumerate(numbers(slot)):
                visible = number <= own if diagonal == a else number < own
                seen.append(visible)
                row = 2 * a + h
                new = jnp.maximum(new, jnp.where(visible, peaks[block][row : row + 1, :], -BIG))
        maxs[block][owner] = new
        fade = jnp.exp2(old - new)
        total = sums[block][owner] * fade
        weights = []
        for i, visible in enumerate(seen):
            shift = jnp.where(visible, new, BIG)
            p = jnp.exp2(scores[block][i * SPAN : (i + 1) * SPAN, :] - shift)
            total = total + jnp.sum(p.reshape(SPAN // 8, 8, ROWS), axis=0)
            weights.append(p.astype(BF16))
        values = jnp.concatenate(
            [buf[slot, KROWS + c * WIDTH : KROWS + (c + 1) * WIDTH, :] for slot in slots for c in range(TOK // WIDTH)],
            axis=1,
        )
        product = jnp.dot(values, jnp.concatenate(weights, axis=0), preferred_element_type=F32)
        accs[block][owner] = accs[block][owner] * fade + product
        sums[block][owner] = total

    def single_step(owner, slots, diagonal):
        for block in range(2):
            score_stage(owner, slots, block, diagonal)
        for block in range(2):
            value_stage(owner, slots, block, diagonal)

    def finish(owner, block):
        total = jnp.sum(sums[block][owner], axis=0, keepdims=True)
        return (accs[block][owner] / total).T.astype(BF16)

    barrier = pltpu.get_barrier_semaphore()
    neighbours = [*device.values(), partner]
    for n in neighbours:
        pl.semaphore_signal(barrier, inc=1, device_id=n, device_id_type=LOGICAL)
    spread_keys()
    pl.semaphore_wait(barrier, len(neighbours))

    forward([(0, 0)])
    qf[...] = q_ref[...].astype(F32)
    for block in range(2):
        for h in range(GROUP):
            qs[block, h * SPAN : (h + 1) * SPAN, :] = head(other, block, h).astype(BF16)
        z_copy(block).start()
    z_copy(2).start()
    for block in range(2):
        for h in range(GROUP):
            spread(head(z, block, h), 0, block, h)
        accs[block][...] = jnp.zeros_like(accs[block])
        sums[block][...] = jnp.zeros_like(sums[block])
        maxs[block][...] = jnp.full(maxs[block].shape, -BIG, F32)
    single_step(0, [0], 0)
    arrive([(0, n) for n in range(1, 5)])

    def place_of(t):
        owner, pair, begin = jnp.int32(0), t, 0
        for own, first, pairs in RUNS:
            owner = jnp.where(t >= begin, own, owner)
            pair = jnp.where(t >= begin, t - begin + first, pair)
            begin += pairs
        return owner, [2 * pair, 2 * pair + 1]

    def queries_come(block):
        z_copy(block).wait_recv()
        ids[1, block] = qz[block, ROWS:, :].astype(F32)[0:8]
        for h in range(GROUP):
            spread(qz[block, h * SPAN : (h + 1) * SPAN, :].astype(F32), 1, block, h)

    def keys_come():
        z_copy(2).wait_recv()
        forward([(1, 0)])

    def diagonal_meets():
        single_step(0, [1], None)
        single_step(1, [0, 1], 1)
        owner, slots = place_of(jnp.int32(DIAGONAL_AT))
        score_stage(owner, slots, 0)

    def outputs_go():
        for block in range(2):
            oz[block] = finish(1, block)
        z_copy(3).start()

    events = {at: [lambda units=units: arrive(units)] for at, units in SERVICE.items()}
    for at, event in (
        (QUERIES_AT, lambda: queries_come(0)),
        (QUERIES_AT + 1, lambda: queries_come(1)),
        (KEYS_AT, keys_come),
        (DIAGONAL_AT, diagonal_meets),
        (OUTPUT_AT, outputs_go),
    ):
        events.setdefault(at, []).insert(0, event)
    starts = sorted(events)

    def step(t, carry):
        owner, slots = place_of(t)
        owner2, slots2 = place_of(jnp.minimum(t + 1, STEPS - 1))
        score_stage(owner, slots, 1)
        value_stage(owner, slots, 0)
        score_stage(owner2, slots2, 0)
        value_stage(owner, slots, 1)
        return carry

    def stretch(e, carry):
        begin, end = jnp.int32(0), jnp.int32(STEPS)
        for i, at in enumerate(starts):
            begin = jnp.where(e == i + 1, at, begin)
            end = jnp.where(e == i, at, end)

            @pl.when(e == i + 1)
            def _(at=at):
                for event in events[at]:
                    event()

        return lax.fori_loop(begin, end, step, carry)

    score_stage(0, [2, 3], 0)
    lax.fori_loop(0, len(starts) + 1, stretch, 0)
    for block in range(2):
        o_ref[z, block] = finish(0, block)
    z_copy(3).wait_recv()
    for i in range(4):
        z_copy(i).wait_send()
    for wave in range(2):
        sent = buf.at[0 : UNITS - 1]
        copy(sent, sent, send_sem.at[wave], recv_sem.at[wave, 0], partner).wait_send()


def attend(q, k, v, positions):
    scratch = [
        pltpu.VMEM((2 * UNITS, UROWS, WIDTH), BF16),
        pltpu.VMEM((UROWS, WIDTH), BF16),
        pltpu.VMEM((2, 2, ROWS, 2 * WIDTH), BF16),
        pltpu.VMEM((2, ROWS + 16, WIDTH), BF16),
        pltpu.VMEM((2, ROWS + 16, WIDTH), BF16),
        pltpu.VMEM((2, ROWS, WIDTH), BF16),
        pltpu.VMEM(q.shape, F32),
        pltpu.VMEM(k.shape, F32),
        pltpu.VMEM(v.shape, F32),
        pltpu.VMEM((2, 2, 8, WIDTH), F32),
    ]
    for shape in [(2, WIDTH, ROWS)] * 2 + [(2, 1, ROWS)] * 2 + [(2, 8, ROWS)] * 2 + [(2 * TOK, ROWS)] * 2 + [(8, ROWS)] * 2:
        scratch.append(pltpu.VMEM(shape, F32))
    scratch += [
        pltpu.SemaphoreType.DMA((2,)),
        pltpu.SemaphoreType.DMA((2, UNITS)),
        pltpu.SemaphoreType.DMA((4,)),
        pltpu.SemaphoreType.DMA((4,)),
    ]
    return pl.pallas_call(
        kernel,
        out_shape=jax.ShapeDtypeStruct((2, 2, ROWS, WIDTH), BF16),
        in_specs=[pl.BlockSpec(memory_space=pltpu.VMEM)] * 3 + [pl.BlockSpec(memory_space=pltpu.SMEM)],
        out_specs=pl.BlockSpec(memory_space=pltpu.VMEM),
        scratch_shapes=scratch,
        compiler_params=pltpu.CompilerParams(collective_id=0, has_side_effects=True, vmem_limit_bytes=56 << 20),
    )(q, k, v, positions)


def body(queries, keys, values, positions):
    rows = [a.reshape(-1, WIDTH) for a in (queries, keys, values)]
    out = attend(*rows, positions).reshape(2, 2, GROUP, SPAN, WIDTH)
    return out.transpose(1, 3, 0, 2, 4).reshape(TOK, 2 * GROUP, WIDTH)


def solution(mesh):
    return jax.shard_map(
        body,
        mesh=mesh,
        in_specs=(P("cp", "tp", None), P("cp", "tp", None), P("cp", "tp", None), P("cp")),
        out_specs=P("cp", "tp", None),
        check_vma=False,
    )
```

```python
import jax
import jax.numpy as jnp
from jax import lax
from jax.experimental import pallas as pl
from jax.experimental.pallas import tpu as pltpu
from jax.sharding import PartitionSpec as P

LOGICAL = pl.DeviceIdType.LOGICAL
F32 = jnp.float32
BF16 = jnp.bfloat16

SPAN = 192
TOK = 2 * SPAN
GROUP = 4
WIDTH = 128
ROWS = GROUP * SPAN
KROWS = TOK + 16
UROWS = KROWS + TOK
BIG = 3.4028235e38
SCALE = WIDTH**-0.5 * 1.4426950408889634

ORDER = [
    (0, 0),
    (-1, 0), (1, 0), (0, -1), (0, 1),
    (2, 0), (0, 2),
    (-1, -1), (1, 1), (-1, 1), (1, -1),
    (2, -1), (-1, 2), (2, 1), (1, 2),
    (2, 2),
]
UNITS = len(ORDER)
PAIRS = [[(0, 0), (1, 0)]]
for _wave in range(2):
    for _unit in range(1, 15, 2):
        PAIRS.append([(_wave, _unit), (_wave, _unit + 1)])
PAIRS.append([(0, 15), (1, 15)])
SLOT = {unit: 2 * r + a for r, pair in enumerate(PAIRS) for a, unit in enumerate(pair)}

RUNS = [
    (0, 1, 2), (1, 1, 2), (0, 3, 1), (1, 3, 1), (0, 4, 2), (1, 4, 2), (0, 6, 2), (1, 6, 2),
    (1, 8, 4), (0, 8, 1), (1, 12, 4), (0, 9, 7),
]
STEPS = sum(run[2] for run in RUNS)
SERVICE = {
    3: [(0, 5), (0, 6)],
    4: [(0, 7), (0, 8), (0, 9), (0, 10)],
    7: [(1, 1), (1, 2), (1, 3), (1, 4)],
    8: [(0, 11), (0, 12), (0, 13), (0, 14)],
    11: [(0, 15), (1, 5), (1, 6)],
    13: [(1, 7), (1, 8), (1, 9), (1, 10)],
    17: [(1, 11), (1, 12), (1, 13), (1, 14)],
    20: [(1, 15)],
}
QUERIES_AT = 1
KEYS_AT = 4
DIAGONAL_AT = 6
OUTPUT_AT = 23


def wrap(d):
    return (d + 1) % 4 - 1


def forwards(wave, kind, n):
    place = ORDER[n]
    first, second = (0, 1) if kind == 0 else (1, 0)
    sends = []

    def send(axis, direction):
        there = list(place)
        there[axis] = wrap(there[axis] - direction)
        sends.append((axis, direction, ORDER.index(tuple(there))))

    around = 1 if wave == 0 else -1
    if place[second] == 0:
        if place[first] == 0:
            send(first, 1)
            send(first, -1)
        elif place[first] == -around:
            send(first, around)
        send(second, 1)
        send(second, -1)
    else:
        way = -1 if place[first] in (0, around) else 1
        if place[second] == -way:
            send(second, way)
    return sends


def kernel(
    q_ref, k_ref, v_ref, p_ref, o_ref,
    buf, kvz, qx, qs, qz, oz, qf, kf, vf, ids,
    acc0, acc1, m0, m1, l0, l1, s0, s1, c0, c1,
    send_sem, recv_sem, zsend_sem, zrecv_sem,
):
    accs, maxs, sums = (acc0, acc1), (m0, m1), (l0, l1)
    scores, peaks = (s0, s1), (c0, c1)
    cp = lax.axis_index("cp")
    y, x, z = cp // 8, (cp // 2) % 4, cp % 2
    other = 1 - z

    base = lax.axis_index("tp") * 32 + z
    device = {
        (0, 1): base + (y * 4 + (x + 1) % 4) * 2,
        (0, -1): base + (y * 4 + (x + 3) % 4) * 2,
        (1, 1): base + (((y + 1) % 4) * 4 + x) * 2,
        (1, -1): base + (((y + 3) % 4) * 4 + x) * 2,
    }
    partner = base + (y * 4 + x) * 2 + other - z

    def rows(kind):
        return slice(0, KROWS) if kind == 0 else slice(KROWS, UROWS)

    def copy(src, dst, ssem, rsem, target):
        return pltpu.make_async_remote_copy(
            src_ref=src,
            dst_ref=dst,
            send_sem=ssem,
            recv_sem=rsem,
            device_id=target,
            device_id_type=LOGICAL,
        )

    def forward(units):
        sends = [(*send, kind, wave, n) for wave, n in units for kind in range(2) for send in forwards(wave, kind, n)]
        for axis, direction, there, kind, wave, n in sorted(sends, key=lambda send: send[2]):
            copy(
                buf.at[SLOT[(wave, n)], rows(kind)],
                buf.at[SLOT[(wave, there)], rows(kind)],
                send_sem.at[wave],
                recv_sem.at[wave, there],
                device[axis, direction],
            ).start()

    def arrive(units):
        for wave, n in units:
            here = buf.at[SLOT[(wave, n)]]
            copy(here, here, send_sem.at[wave], recv_sem.at[wave, n], partner).wait_recv()
        forward(units)

    def z_copy(i):
        src, dst = (
            (qs.at[0], qz.at[0]),
            (qs.at[1], qz.at[1]),
            (kvz, buf.at[SLOT[(1, 0)]]),
            (oz, o_ref.at[z]),
        )[i]
        return copy(src, dst, zsend_sem.at[i], zrecv_sem.at[i], partner)

    def spread(q, owner, block, h):
        q = q * SCALE
        high = q.astype(BF16)
        rows = slice(h * SPAN, (h + 1) * SPAN)
        qx[owner, block, rows, 0:WIDTH] = high
        qx[owner, block, rows, WIDTH : 2 * WIDTH] = (q - high.astype(F32)).astype(BF16)

    def head(owner_z, block, h):
        return qf[pl.ds(block * SPAN * 2 * GROUP + GROUP * owner_z + h, SPAN, stride=2 * GROUP), :]

    def spread_keys():
        kf[...] = k_ref[...].astype(F32)
        vf[...] = v_ref[...].astype(F32)
        blocks = [jnp.full((8, WIDTH), p_ref[b * SPAN] // SPAN, jnp.int32).astype(F32) for b in range(2)]
        for b in range(2):
            ids[0, b] = blocks[b]
            qs[b, ROWS:, :] = jnp.concatenate([blocks[b]] * 2, axis=0).astype(BF16)
        for served, put in ((z, buf.at[0]), (other, kvz)):
            put[0:TOK, :] = kf[pl.ds(served, TOK, stride=2), :].astype(BF16)
            put[TOK:KROWS, :] = jnp.concatenate(blocks, axis=0).astype(BF16)
            for c in range(TOK // WIDTH):
                v = vf[pl.ds(2 * WIDTH * c + served, WIDTH, stride=2), :]
                put[KROWS + c * WIDTH : KROWS + (c + 1) * WIDTH, :] = v.T.astype(BF16)

    def wide(tile):
        return jnp.concatenate([tile[0:1]] * (ROWS // WIDTH), axis=1)

    def numbers(slot):
        tile = buf[slot, TOK:KROWS, :].astype(F32)
        return [wide(tile[8 * h : 8 * h + 8]) for h in range(2)]

    def score_stage(owner, slots, block, diagonal=None):
        q = qx[owner, block]
        for a, slot in enumerate(slots):
            keys = buf[slot, 0:TOK, :]
            s = lax.dot_general(
                jnp.concatenate([keys, keys], axis=1), q, (((1,), (1,)), ((), ())), preferred_element_type=F32
            )
            for h in range(2):
                sh = s[h * SPAN : (h + 1) * SPAN]
                if diagonal == a and h == block:
                    key_off = lax.broadcasted_iota(jnp.int32, (SPAN, SPAN), 0)
                    query_off = lax.broadcasted_iota(jnp.int32, (SPAN, SPAN), 1)
                    seen = jnp.where(key_off <= query_off, 0.0, -BIG).astype(F32)
                    sh = sh + jnp.concatenate([seen] * GROUP, axis=1)
                at = a * TOK + h * SPAN
                scores[block][at : at + SPAN, :] = sh
                top = jnp.max(sh.reshape(SPAN // 8, 8, ROWS), axis=0)
                peaks[block][2 * a + h : 2 * a + h + 1, :] = jnp.max(top, axis=0, keepdims=True)

    def value_stage(owner, slots, block, diagonal=None):
        own = wide(ids[owner, block])
        old = maxs[block][owner]
        new = old
        seen = []
        for a, slot in enumerate(slots):
            for h, number in enumerate(numbers(slot)):
                visible = number <= own if diagonal == a else number < own
                seen.append(visible)
                row = 2 * a + h
                new = jnp.maximum(new, jnp.where(visible, peaks[block][row : row + 1, :], -BIG))
        maxs[block][owner] = new
        fade = jnp.exp2(old - new)
        total = sums[block][owner] * fade
        weights = []
        for i, visible in enumerate(seen):
            shift = jnp.where(visible, new, BIG)
            p = jnp.exp2(scores[block][i * SPAN : (i + 1) * SPAN, :] - shift)
            total = total + jnp.sum(p.reshape(SPAN // 8, 8, ROWS), axis=0)
            weights.append(p.astype(BF16))
        values = jnp.concatenate(
            [buf[slot, KROWS + c * WIDTH : KROWS + (c + 1) * WIDTH, :] for slot in slots for c in range(TOK // WIDTH)],
            axis=1,
        )
        product = jnp.dot(values, jnp.concatenate(weights, axis=0), preferred_element_type=F32)
        accs[block][owner] = accs[block][owner] * fade + product
        sums[block][owner] = total

    def single_step(owner, slots, diagonal):
        for block in range(2):
            score_stage(owner, slots, block, diagonal)
        for block in range(2):
            value_stage(owner, slots, block, diagonal)

    def finish(owner, block):
        total = jnp.sum(sums[block][owner], axis=0, keepdims=True)
        return (accs[block][owner] / total).T.astype(BF16)

    barrier = pltpu.get_barrier_semaphore()
    neighbours = [*device.values(), partner]
    for n in neighbours:
        pl.semaphore_signal(barrier, inc=1, device_id=n, device_id_type=LOGICAL)
    spread_keys()
    pl.semaphore_wait(barrier, len(neighbours))

    forward([(0, 0)])
    qf[...] = q_ref[...].astype(F32)
    for block in range(2):
        for h in range(GROUP):
            qs[block, h * SPAN : (h + 1) * SPAN, :] = head(other, block, h).astype(BF16)
        z_copy(block).start()
    z_copy(2).start()
    for block in range(2):
        for h in range(GROUP):
            spread(head(z, block, h), 0, block, h)
        accs[block][...] = jnp.zeros_like(accs[block])
        sums[block][...] = jnp.zeros_like(sums[block])
        maxs[block][...] = jnp.full(maxs[block].shape, -BIG, F32)
    single_step(0, [0], 0)
    arrive([(0, n) for n in range(1, 5)])

    def place_of(t):
        owner, pair, begin = jnp.int32(0), t, 0
        for own, first, pairs in RUNS:
            owner = jnp.where(t >= begin, own, owner)
            pair = jnp.where(t >= begin, t - begin + first, pair)
            begin += pairs
        return owner, [2 * pair, 2 * pair + 1]

    def queries_come(block):
        z_copy(block).wait_recv()
        ids[1, block] = qz[block, ROWS:, :].astype(F32)[0:8]
        for h in range(GROUP):
            spread(qz[block, h * SPAN : (h + 1) * SPAN, :].astype(F32), 1, block, h)

    def keys_come():
        z_copy(2).wait_recv()
        forward([(1, 0)])

    def diagonal_meets():
        single_step(0, [1], None)
        single_step(1, [0, 1], 1)
        owner, slots = place_of(jnp.int32(DIAGONAL_AT))
        score_stage(owner, slots, 0)

    def outputs_go():
        for block in range(2):
            oz[block] = finish(1, block)
        z_copy(3).start()

    events = {at: [lambda units=units: arrive(units)] for at, units in SERVICE.items()}
    for at, event in (
        (QUERIES_AT, lambda: queries_come(0)),
        (QUERIES_AT + 1, lambda: queries_come(1)),
        (KEYS_AT, keys_come),
        (DIAGONAL_AT, diagonal_meets),
        (OUTPUT_AT, outputs_go),
    ):
        events.setdefault(at, []).insert(0, event)
    starts = sorted(events)

    def step(t, carry):
        owner, slots = place_of(t)
        owner2, slots2 = place_of(jnp.minimum(t + 1, STEPS - 1))
        score_stage(owner, slots, 1)
        value_stage(owner, slots, 0)
        score_stage(owner2, slots2, 0)
        value_stage(owner, slots, 1)
        return carry

    def stretch(e, carry):
        begin, end = jnp.int32(0), jnp.int32(STEPS)
        for i, at in enumerate(starts):
            begin = jnp.where(e == i + 1, at, begin)
            end = jnp.where(e == i, at, end)

            @pl.when(e == i + 1)
            def _(at=at):
                for event in events[at]:
                    event()

        return lax.fori_loop(begin, end, step, carry)

    score_stage(0, [2, 3], 0)
    lax.fori_loop(0, len(starts) + 1, stretch, 0)
    for block in range(2):
        o_ref[z, block] = finish(0, block)
    z_copy(3).wait_recv()
    for i in range(4):
        z_copy(i).wait_send()
    for wave in range(2):
        sent = buf.at[0 : UNITS - 1]
        copy(sent, sent, send_sem.at[wave], recv_sem.at[wave, 0], partner).wait_send()


def attend(q, k, v, positions):
    scratch = [
        pltpu.VMEM((2 * UNITS, UROWS, WIDTH), BF16),
        pltpu.VMEM((UROWS, WIDTH), BF16),
        pltpu.VMEM((2, 2, ROWS, 2 * WIDTH), BF16),
        pltpu.VMEM((2, ROWS + 16, WIDTH), BF16),
        pltpu.VMEM((2, ROWS + 16, WIDTH), BF16),
        pltpu.VMEM((2, ROWS, WIDTH), BF16),
        pltpu.VMEM(q.shape, F32),
        pltpu.VMEM(k.shape, F32),
        pltpu.VMEM(v.shape, F32),
        pltpu.VMEM((2, 2, 8, WIDTH), F32),
    ]
    for shape in [(2, WIDTH, ROWS)] * 2 + [(2, 1, ROWS)] * 2 + [(2, 8, ROWS)] * 2 + [(2 * TOK, ROWS)] * 2 + [(8, ROWS)] * 2:
        scratch.append(pltpu.VMEM(shape, F32))
    scratch += [
        pltpu.SemaphoreType.DMA((2,)),
        pltpu.SemaphoreType.DMA((2, UNITS)),
        pltpu.SemaphoreType.DMA((4,)),
        pltpu.SemaphoreType.DMA((4,)),
    ]
    return pl.pallas_call(
        kernel,
        out_shape=jax.ShapeDtypeStruct((2, 2, ROWS, WIDTH), BF16),
        in_specs=[pl.BlockSpec(memory_space=pltpu.VMEM)] * 3 + [pl.BlockSpec(memory_space=pltpu.SMEM)],
        out_specs=pl.BlockSpec(memory_space=pltpu.VMEM),
        scratch_shapes=scratch,
        compiler_params=pltpu.CompilerParams(collective_id=0, has_side_effects=True, vmem_limit_bytes=56 << 20),
    )(q, k, v, positions)


def body(queries, keys, values, positions):
    rows = [a.reshape(-1, WIDTH) for a in (queries, keys, values)]
    out = attend(*rows, positions).reshape(2, 2, GROUP, SPAN, WIDTH)
    return out.transpose(1, 3, 0, 2, 4).reshape(TOK, 2 * GROUP, WIDTH)


def solution(mesh):
    return jax.shard_map(
        body,
        mesh=mesh,
        in_specs=(P("cp", "tp", None), P("cp", "tp", None), P("cp", "tp", None), P("cp")),
        out_specs=P("cp", "tp", None),
        check_vma=False,
    )
```

```python
import jax
import jax.numpy as jnp
from jax import lax
from jax.experimental import pallas as pl
from jax.experimental.pallas import tpu as pltpu
from jax.sharding import PartitionSpec as P

LOGICAL = pl.DeviceIdType.LOGICAL
F32 = jnp.float32
BF16 = jnp.bfloat16

SPAN = 192
TOK = 2 * SPAN
GROUP = 4
WIDTH = 128
ROWS = GROUP * SPAN
KROWS = TOK + 16
UROWS = KROWS + TOK
BIG = 3.4028235e38
SCALE = WIDTH**-0.5 * 1.4426950408889634

ORDER = [
    (0, 0),
    (-1, 0), (1, 0), (0, -1), (0, 1),
    (2, 0), (0, 2),
    (-1, -1), (1, 1), (-1, 1), (1, -1),
    (2, -1), (-1, 2), (2, 1), (1, 2),
    (2, 2),
]
UNITS = len(ORDER)
PAIRS = [[(0, 0), (1, 0)]]
for _wave in range(2):
    for _unit in range(1, 15, 2):
        PAIRS.append([(_wave, _unit), (_wave, _unit + 1)])
PAIRS.append([(0, 15), (1, 15)])
SLOT = {unit: 2 * r + a for r, pair in enumerate(PAIRS) for a, unit in enumerate(pair)}

RUNS = [
    (0, 1, 2), (1, 1, 2), (0, 3, 1), (1, 3, 1), (0, 4, 2), (1, 4, 2), (0, 6, 2), (1, 6, 2),
    (1, 8, 4), (0, 8, 1), (1, 12, 4), (0, 9, 7),
]
STEPS = sum(run[2] for run in RUNS)
SERVICE = {
    3: [(0, 5), (0, 6)],
    4: [(0, 7), (0, 8), (0, 9), (0, 10)],
    7: [(1, 1), (1, 2), (1, 3), (1, 4)],
    8: [(0, 11), (0, 12), (0, 13), (0, 14)],
    11: [(0, 15), (1, 5), (1, 6)],
    13: [(1, 7), (1, 8), (1, 9), (1, 10)],
    17: [(1, 11), (1, 12), (1, 13), (1, 14)],
    20: [(1, 15)],
}
QUERIES_AT = 1
KEYS_AT = 4
DIAGONAL_AT = 6
OUTPUT_AT = 23


def wrap(d):
    return (d + 1) % 4 - 1


def forwards(wave, kind, n):
    place = ORDER[n]
    first, second = (0, 1) if kind == 0 else (1, 0)
    sends = []

    def send(axis, direction):
        there = list(place)
        there[axis] = wrap(there[axis] - direction)
        sends.append((axis, direction, ORDER.index(tuple(there))))

    around = 1 if wave == 0 else -1
    if place[second] == 0:
        if place[first] == 0:
            send(first, 1)
            send(first, -1)
        elif place[first] == -around:
            send(first, around)
        send(second, 1)
        send(second, -1)
    else:
        way = -1 if place[first] in (0, around) else 1
        if place[second] == -way:
            send(second, way)
    return sends


def kernel(
    q_ref, k_ref, v_ref, p_ref, o_ref,
    buf, kvz, qx, qs, qz, oz, qf, kf, vf, ids,
    acc0, acc1, m0, m1, l0, l1, s0, s1, c0, c1,
    send_sem, recv_sem, zsend_sem, zrecv_sem,
):
    accs, maxs, sums = (acc0, acc1), (m0, m1), (l0, l1)
    scores, peaks = (s0, s1), (c0, c1)
    cp = lax.axis_index("cp")
    y, x, z = cp // 8, (cp // 2) % 4, cp % 2
    other = 1 - z

    base = lax.axis_index("tp") * 32 + z
    device = {
        (0, 1): base + (y * 4 + (x + 1) % 4) * 2,
        (0, -1): base + (y * 4 + (x + 3) % 4) * 2,
        (1, 1): base + (((y + 1) % 4) * 4 + x) * 2,
        (1, -1): base + (((y + 3) % 4) * 4 + x) * 2,
    }
    partner = base + (y * 4 + x) * 2 + other - z

    def rows(kind):
        return slice(0, KROWS) if kind == 0 else slice(KROWS, UROWS)

    def copy(src, dst, ssem, rsem, target):
        return pltpu.make_async_remote_copy(
            src_ref=src,
            dst_ref=dst,
            send_sem=ssem,
            recv_sem=rsem,
            device_id=target,
            device_id_type=LOGICAL,
        )

    def forward(units):
        sends = [(*send, kind, wave, n) for wave, n in units for kind in range(2) for send in forwards(wave, kind, n)]
        for axis, direction, there, kind, wave, n in sorted(sends, key=lambda send: send[2]):
            copy(
                buf.at[SLOT[(wave, n)], rows(kind)],
                buf.at[SLOT[(wave, there)], rows(kind)],
                send_sem.at[wave],
                recv_sem.at[wave, there],
                device[axis, direction],
            ).start()

    def arrive(units):
        for wave, n in units:
            here = buf.at[SLOT[(wave, n)]]
            copy(here, here, send_sem.at[wave], recv_sem.at[wave, n], partner).wait_recv()
        forward(units)

    def z_copy(i):
        src, dst = (
            (qs.at[0], qz.at[0]),
            (qs.at[1], qz.at[1]),
            (kvz, buf.at[SLOT[(1, 0)]]),
            (oz, o_ref.at[z]),
        )[i]
        return copy(src, dst, zsend_sem.at[i], zrecv_sem.at[i], partner)

    def spread(q, owner, block, h):
        q = q * SCALE
        high = q.astype(BF16)
        rows = slice(h * SPAN, (h + 1) * SPAN)
        qx[owner, block, rows, 0:WIDTH] = high
        qx[owner, block, rows, WIDTH : 2 * WIDTH] = (q - high.astype(F32)).astype(BF16)

    def head(owner_z, block, h):
        return qf[pl.ds(block * SPAN * 2 * GROUP + GROUP * owner_z + h, SPAN, stride=2 * GROUP), :]

    def spread_keys(served, put):
        blocks = [jnp.full((8, WIDTH), p_ref[b * SPAN] // SPAN, jnp.int32).astype(F32) for b in range(2)]
        for b in range(2) if served is z else ():
            ids[0, b] = blocks[b]
            qs[b, ROWS:, :] = jnp.concatenate([blocks[b]] * 2, axis=0).astype(BF16)
        put[0:TOK, :] = kf[pl.ds(served, TOK, stride=2), :].astype(BF16)
        put[TOK:KROWS, :] = jnp.concatenate(blocks, axis=0).astype(BF16)
        for c in range(TOK // WIDTH):
            v = vf[pl.ds(2 * WIDTH * c + served, WIDTH, stride=2), :]
            put[KROWS + c * WIDTH : KROWS + (c + 1) * WIDTH, :] = v.T.astype(BF16)

    def wide(tile):
        return jnp.concatenate([tile[0:1]] * (ROWS // WIDTH), axis=1)

    def numbers(slot):
        tile = buf[slot, TOK:KROWS, :].astype(F32)
        return [wide(tile[8 * h : 8 * h + 8]) for h in range(2)]

    def score_stage(owner, slots, block, diagonal=None):
        q = qx[owner, block]
        for a, slot in enumerate(slots):
            keys = buf[slot, 0:TOK, :]
            s = lax.dot_general(
                jnp.concatenate([keys, keys], axis=1), q, (((1,), (1,)), ((), ())), preferred_element_type=F32
            )
            for h in range(2):
                sh = s[h * SPAN : (h + 1) * SPAN]
                if diagonal == a and h == block:
                    key_off = lax.broadcasted_iota(jnp.int32, (SPAN, SPAN), 0)
                    query_off = lax.broadcasted_iota(jnp.int32, (SPAN, SPAN), 1)
                    seen = jnp.where(key_off <= query_off, 0.0, -BIG).astype(F32)
                    sh = sh + jnp.concatenate([seen] * GROUP, axis=1)
                at = a * TOK + h * SPAN
                scores[block][at : at + SPAN, :] = sh
                top = jnp.max(sh.reshape(SPAN // 8, 8, ROWS), axis=0)
                peaks[block][2 * a + h : 2 * a + h + 1, :] = jnp.max(top, axis=0, keepdims=True)

    def value_stage(owner, slots, block, diagonal=None):
        own = wide(ids[owner, block])
        old = maxs[block][owner]
        new = old
        seen = []
        for a, slot in enumerate(slots):
            for h, number in enumerate(numbers(slot)):
                visible = number <= own if diagonal == a else number < own
                seen.append(visible)
                row = 2 * a + h
                new = jnp.maximum(new, jnp.where(visible, peaks[block][row : row + 1, :], -BIG))
        maxs[block][owner] = new
        fade = jnp.exp2(old - new)
        total = sums[block][owner] * fade
        weights = []
        for i, visible in enumerate(seen):
            shift = jnp.where(visible, new, BIG)
            p = jnp.exp2(scores[block][i * SPAN : (i + 1) * SPAN, :] - shift)
            total = total + jnp.sum(p.reshape(SPAN // 8, 8, ROWS), axis=0)
            weights.append(p.astype(BF16))
        values = jnp.concatenate(
            [buf[slot, KROWS + c * WIDTH : KROWS + (c + 1) * WIDTH, :] for slot in slots for c in range(TOK // WIDTH)],
            axis=1,
        )
        product = jnp.dot(values, jnp.concatenate(weights, axis=0), preferred_element_type=F32)
        accs[block][owner] = accs[block][owner] * fade + product
        sums[block][owner] = total

    def single_step(owner, slots, diagonal):
        for block in range(2):
            score_stage(owner, slots, block, diagonal)
        for block in range(2):
            value_stage(owner, slots, block, diagonal)

    def finish(owner, block):
        total = jnp.sum(sums[block][owner], axis=0, keepdims=True)
        return (accs[block][owner] / total).T.astype(BF16)

    barrier = pltpu.get_barrier_semaphore()
    neighbours = [*device.values(), partner]
    for n in neighbours:
        pl.semaphore_signal(barrier, inc=1, device_id=n, device_id_type=LOGICAL)
    kf[...] = k_ref[...].astype(F32)
    vf[...] = v_ref[...].astype(F32)
    spread_keys(z, buf.at[0])
    pl.semaphore_wait(barrier, len(neighbours))

    forward([(0, 0)])
    qf[...] = q_ref[...].astype(F32)
    for block in range(2):
        for h in range(GROUP):
            qs[block, h * SPAN : (h + 1) * SPAN, :] = head(other, block, h).astype(BF16)
        z_copy(block).start()
    spread_keys(other, kvz)
    z_copy(2).start()
    for block in range(2):
        for h in range(GROUP):
            spread(head(z, block, h), 0, block, h)
        accs[block][...] = jnp.zeros_like(accs[block])
        sums[block][...] = jnp.zeros_like(sums[block])
        maxs[block][...] = jnp.full(maxs[block].shape, -BIG, F32)
    single_step(0, [0], 0)
    arrive([(0, n) for n in range(1, 5)])

    def place_of(t):
        owner, pair, begin = jnp.int32(0), t, 0
        for own, first, pairs in RUNS:
            owner = jnp.where(t >= begin, own, owner)
            pair = jnp.where(t >= begin, t - begin + first, pair)
            begin += pairs
        return owner, [2 * pair, 2 * pair + 1]

    def queries_come(block):
        z_copy(block).wait_recv()
        ids[1, block] = qz[block, ROWS:, :].astype(F32)[0:8]
        for h in range(GROUP):
            spread(qz[block, h * SPAN : (h + 1) * SPAN, :].astype(F32), 1, block, h)

    def keys_come():
        z_copy(2).wait_recv()
        forward([(1, 0)])

    def diagonal_meets():
        single_step(0, [1], None)
        single_step(1, [0, 1], 1)
        owner, slots = place_of(jnp.int32(DIAGONAL_AT))
        score_stage(owner, slots, 0)

    def outputs_go():
        for block in range(2):
            oz[block] = finish(1, block)
        z_copy(3).start()

    events = {at: [lambda units=units: arrive(units)] for at, units in SERVICE.items()}
    for at, event in (
        (QUERIES_AT, lambda: queries_come(0)),
        (QUERIES_AT + 1, lambda: queries_come(1)),
        (KEYS_AT, keys_come),
        (DIAGONAL_AT, diagonal_meets),
        (OUTPUT_AT, outputs_go),
    ):
        events.setdefault(at, []).insert(0, event)
    starts = sorted(events)

    def step(t, carry):
        owner, slots = place_of(t)
        owner2, slots2 = place_of(jnp.minimum(t + 1, STEPS - 1))
        score_stage(owner, slots, 1)
        value_stage(owner, slots, 0)
        score_stage(owner2, slots2, 0)
        value_stage(owner, slots, 1)
        return carry

    def stretch(e, carry):
        begin, end = jnp.int32(0), jnp.int32(STEPS)
        for i, at in enumerate(starts):
            begin = jnp.where(e == i + 1, at, begin)
            end = jnp.where(e == i, at, end)

            @pl.when(e == i + 1)
            def _(at=at):
                for event in events[at]:
                    event()

        return lax.fori_loop(begin, end, step, carry)

    score_stage(0, [2, 3], 0)
    lax.fori_loop(0, len(starts) + 1, stretch, 0)
    for block in range(2):
        o_ref[z, block] = finish(0, block)
    z_copy(3).wait_recv()
    for i in range(4):
        z_copy(i).wait_send()
    for wave in range(2):
        sent = buf.at[0 : UNITS - 1]
        copy(sent, sent, send_sem.at[wave], recv_sem.at[wave, 0], partner).wait_send()


def attend(q, k, v, positions):
    scratch = [
        pltpu.VMEM((2 * UNITS, UROWS, WIDTH), BF16),
        pltpu.VMEM((UROWS, WIDTH), BF16),
        pltpu.VMEM((2, 2, ROWS, 2 * WIDTH), BF16),
        pltpu.VMEM((2, ROWS + 16, WIDTH), BF16),
        pltpu.VMEM((2, ROWS + 16, WIDTH), BF16),
        pltpu.VMEM((2, ROWS, WIDTH), BF16),
        pltpu.VMEM(q.shape, F32),
        pltpu.VMEM(k.shape, F32),
        pltpu.VMEM(v.shape, F32),
        pltpu.VMEM((2, 2, 8, WIDTH), F32),
    ]
    for shape in [(2, WIDTH, ROWS)] * 2 + [(2, 1, ROWS)] * 2 + [(2, 8, ROWS)] * 2 + [(2 * TOK, ROWS)] * 2 + [(8, ROWS)] * 2:
        scratch.append(pltpu.VMEM(shape, F32))
    scratch += [
        pltpu.SemaphoreType.DMA((2,)),
        pltpu.SemaphoreType.DMA((2, UNITS)),
        pltpu.SemaphoreType.DMA((4,)),
        pltpu.SemaphoreType.DMA((4,)),
    ]
    return pl.pallas_call(
        kernel,
        out_shape=jax.ShapeDtypeStruct((2, 2, ROWS, WIDTH), BF16),
        in_specs=[pl.BlockSpec(memory_space=pltpu.VMEM)] * 3 + [pl.BlockSpec(memory_space=pltpu.SMEM)],
        out_specs=pl.BlockSpec(memory_space=pltpu.VMEM),
        scratch_shapes=scratch,
        compiler_params=pltpu.CompilerParams(collective_id=0, has_side_effects=True, vmem_limit_bytes=56 << 20),
    )(q, k, v, positions)


def body(queries, keys, values, positions):
    rows = [a.reshape(-1, WIDTH) for a in (queries, keys, values)]
    out = attend(*rows, positions).reshape(2, 2, GROUP, SPAN, WIDTH)
    return out.transpose(1, 3, 0, 2, 4).reshape(TOK, 2 * GROUP, WIDTH)


def solution(mesh):
    return jax.shard_map(
        body,
        mesh=mesh,
        in_specs=(P("cp", "tp", None), P("cp", "tp", None), P("cp", "tp", None), P("cp")),
        out_specs=P("cp", "tp", None),
        check_vma=False,
    )
```
